32 devices in a mesh: parts: 2 (over y), rows: 4 (over z), cols: 2 (over x), layers: 2 (over core).
Axes of the slice: x: 2, y: 2, z: 4, core: 2. Of those that a mesh axis runs over, the one named last changes fastest.
Arguments:
- a_blocks: float32 [8, 2, 2, 32, 128, 128], P(('parts', 'rows'), 'cols', 'layers'), parts along dimension 0, may hold values from -6 to 6
- a_rows: int32 [8, 2, 2, 32], P(('parts', 'rows'), 'cols', 'layers'), parts along dimension 0, may hold values from 0 to 7
- b_blocks: float32 [8, 2, 2, 8, 128, 128], P(('parts', 'rows'), 'cols', 'layers'), parts along dimension 0, may hold values from -0.5 to 0.5
- b_cols: int32 [8, 2, 2, 8], P(('parts', 'rows'), 'cols', 'layers'), parts along dimension 0, may hold values from 0 to 7
- pairs: int32 [8, 2, 2, 2, 2, 96], P(('parts', 'rows'), 'cols', 'layers'), parts along dimension 0, may hold values from 0 to 31, as said below
- counts: int32 [8, 2, 2, 2], P(('parts', 'rows'), 'cols', 'layers'), parts along dimension 0, may hold values from 1 to 96, as said below
- kept: int32 [8, 2, 8, 8], P(('parts', 'rows'), 'cols'), parts along dimension 0, may hold values from -1 to 47, as said below
Outputs:
- c_blocks: float32 [8, 2, 48, 128, 128], P(('parts', 'rows'), 'cols', 'layers'), parts along dimension 0
The draws below stay inside these ranges and needn't reach their ends.
There are 2 independent parts, one for each index of `parts`. The reference program is written for one: setup_inputs(seed, part) draws one part's arguments, and reference() takes and returns one part's arrays. A program takes and returns all parts, laid end to end along the dimension named above; each array names one. Nothing has to cross between parts.
Inputs may be any that keep to these rules, and one draw needn't show every extreme that they name: In each list the pairs are distinct and meet in shared inner block indices of the two panels; the first entry indexes the 32 A blocks, the second the 8 B blocks. `counts`: some list is full in every draw. `kept`: in each tile every slot 0 to 47 stands exactly once; all other entries are -1.
All inputs are finite; a program needn't handle non-finite values.
Results may differ from the reference program's by a relative error of at most 0.0003.
Values sent between devices are 32-bit elements; how exact they have to be, the bound alone decides.
A program may use at most 64 MiB of HBM per device.

```python
import jax
import jax.numpy as jnp
from jax import lax

BLOCK = 128
A_BLOCKS = 32
B_BLOCKS = 8
PAIRS = 96
TILE_ROWS = 8
TILE_COLS = 8
KEPT = 48
N_ROWS = 4
N_COLS = 2
N_LAYERS = 2


def inner_labels(key, panel_count, block_count):
    keys = jax.random.split(key, panel_count)
    base = jnp.arange(block_count, dtype=jnp.int32) % 2

    def one_panel(subkey):
        return jax.random.permutation(subkey, base)
    return jax.vmap(one_panel)(keys)


def draw_pairs(key, part):
    key = jax.random.fold_in(key, 11)
    a_key, b_key, order_key = jax.random.split(key, 3)
    panel_count = N_ROWS * N_COLS * N_LAYERS
    a_inner = inner_labels(a_key, panel_count, A_BLOCKS).reshape(N_ROWS, N_COLS, N_LAYERS, A_BLOCKS)
    b_inner = inner_labels(b_key, panel_count, B_BLOCKS).reshape(N_ROWS, N_COLS, N_LAYERS, B_BLOCKS)
    grid_rows = jnp.arange(N_ROWS, dtype=jnp.int32)
    grid_cols = jnp.arange(N_COLS, dtype=jnp.int32)
    step_lists = []
    for step_pos in range(2):
        a_from = a_inner[(grid_rows - step_pos) % N_ROWS]
        b_from = b_inner[:, (grid_cols - step_pos) % N_COLS]
        step_lists.append((a_from, b_from))
    list_count = N_ROWS * N_COLS * N_LAYERS * 2
    a_all = jnp.stack([item[0] for item in step_lists], axis=3).reshape(list_count, A_BLOCKS)
    b_all = jnp.stack([item[1] for item in step_lists], axis=3).reshape(list_count, B_BLOCKS)
    keys = jax.random.split(order_key, list_count)
    total = A_BLOCKS * B_BLOCKS
    pair_iota = jnp.arange(total, dtype=jnp.int32)

    def one_list(subkey, a_label, b_label):
        first_key, second_key = jax.random.split(subkey)
        label_rank = jax.random.permutation(first_key, jnp.arange(2, dtype=jnp.int32))
        tie_break = jax.random.permutation(second_key, pair_iota)
        a_part = pair_iota // B_BLOCKS
        b_part = pair_iota % B_BLOCKS
        a_side = a_label[a_part]
        match = a_side == b_label[b_part]
        score = jnp.where(match, label_rank[a_side] * total + tie_break, 4 * total + tie_break)
        order = jnp.argsort(score, stable=True)[:PAIRS]
        return jnp.stack([order // B_BLOCKS, order % B_BLOCKS]).astype(jnp.int32)
    return jax.vmap(one_list)(keys, a_all, b_all).reshape(N_ROWS, N_COLS, N_LAYERS, 2, 2, PAIRS)


def draw_counts(key, part):
    key = jax.random.fold_in(key, 12)
    first_key, second_key = jax.random.split(key)
    list_count = N_ROWS * N_COLS * N_LAYERS * 2
    spread = jax.random.randint(first_key, (list_count,), 0, PAIRS + 1)
    values = jnp.maximum(1, spread * spread // PAIRS)
    chosen = jax.random.randint(second_key, (), 0, list_count)
    values = values.at[chosen].set(PAIRS)
    return values.astype(jnp.int32).reshape(N_ROWS, N_COLS, N_LAYERS, 2)


def draw_kept(key, part):
    key = jax.random.fold_in(key, 13)
    keys = jax.random.split(key, N_ROWS * N_COLS)

    def one_tile(subkey):
        order = jax.random.permutation(subkey, TILE_ROWS * TILE_COLS)
        return jnp.where(order < KEPT, order, -1).astype(jnp.int32)
    return jax.vmap(one_tile)(keys).reshape(N_ROWS, N_COLS, TILE_ROWS, TILE_COLS)


def place_ends(drawn, stream_key, smallest, high):
    longest = drawn.shape.index(max(drawn.shape))
    spots = []
    for shift in (0, 1):
        where = [jax.random.randint(jax.random.fold_in(stream_key, axis), (), 0, length) for axis, length in enumerate(drawn.shape)]
        where[longest] = (where[longest] + shift) % drawn.shape[longest]
        spots.append(tuple(where))
    return drawn.at[spots[0]].set(smallest).at[spots[1]].set(high)


def level_of(rng, extent, cuts, least, top_value):
    loudness = 1.0
    for axis_at, blocks in cuts:
        draws = jax.random.uniform(jax.random.fold_in(jax.random.fold_in(rng, 6), axis_at), (blocks,), jnp.float32, least / len(cuts), top_value / len(cuts))
        loudness = loudness * jnp.repeat(jnp.exp(draws), extent[axis_at] // blocks).reshape((-1,) + (1,) * (len(extent) - 1 - axis_at))
    return loudness


def bell_draw(key, extent, width, limit, pieces=(), held_as=jnp.bfloat16):
    array = jax.random.normal(key, extent, jnp.float32) * width
    if len(pieces) > 0:
        array = level_of(key, extent, pieces, -0.22, 0.18) * array
    return jnp.clip(array, min=-limit, max=limit).astype(held_as)


def setup_inputs(seed: int = 0, part: int = 0) -> dict:
    splits = jax.random.split(jax.random.key(seed), 8)
    part_splits = jax.random.split(jax.random.fold_in(splits[7], part), 8)
    a_blocks = bell_draw(part_splits[0], (N_ROWS, N_COLS, N_LAYERS, A_BLOCKS, BLOCK, BLOCK), 1.0, 6.0, ((0, 4), (1, 2), (2, 2)), jnp.float32)
    a_rows = place_ends(jax.random.randint(part_splits[1], (N_ROWS, N_COLS, N_LAYERS, A_BLOCKS), 0, TILE_ROWS), jax.random.fold_in(part_splits[1], 1), 0, TILE_ROWS - 1).astype(jnp.int32)
    b_blocks = bell_draw(part_splits[2], (N_ROWS, N_COLS, N_LAYERS, B_BLOCKS, BLOCK, BLOCK), BLOCK ** -0.5, 0.5, ((0, 4), (1, 2), (2, 2)), jnp.float32)
    b_cols = place_ends(jax.random.randint(part_splits[3], (N_ROWS, N_COLS, N_LAYERS, B_BLOCKS), 0, TILE_COLS), jax.random.fold_in(part_splits[3], 1), 0, TILE_COLS - 1).astype(jnp.int32)
    pairs = draw_pairs(jax.random.fold_in(jax.random.fold_in(splits[7], part), 71), part)
    counts = draw_counts(jax.random.fold_in(jax.random.fold_in(splits[7], part), 71), part)
    kept = draw_kept(jax.random.fold_in(jax.random.fold_in(splits[7], part), 71), part)
    return dict(a_blocks=a_blocks, a_rows=a_rows, b_blocks=b_blocks, b_cols=b_cols, pairs=pairs, counts=counts, kept=kept)


def reference(a_blocks, a_rows, b_blocks, b_cols, pairs, counts, kept):
    def compute_tile(tile_pos):
        row_pos = tile_pos // N_COLS
        col_pos = tile_pos % N_COLS
        slot_table = kept[row_pos, col_pos].reshape(-1)
        running = jnp.zeros((KEPT, BLOCK * BLOCK), jnp.float32)
        pair_iota = jnp.arange(PAIRS, dtype=jnp.int32)
        slot_iota = jnp.arange(KEPT, dtype=jnp.int32)
        for layer_pos in range(N_LAYERS):
            for step_pos in range(2):
                a_source = (row_pos - step_pos) % N_ROWS
                b_source = (col_pos - step_pos) % N_COLS
                a_panel = a_blocks[a_source, col_pos, layer_pos]
                a_panel_rows = a_rows[a_source, col_pos, layer_pos]
                b_panel = b_blocks[row_pos, b_source, layer_pos]
                b_panel_cols = b_cols[row_pos, b_source, layer_pos]
                a_index = pairs[row_pos, col_pos, layer_pos, step_pos, 0]
                b_index = pairs[row_pos, col_pos, layer_pos, step_pos, 1]
                products = jnp.einsum("pik,pkj->pij", a_panel[a_index], b_panel[b_index],
                                      precision=lax.Precision.HIGHEST)
                cell_index = a_panel_rows[a_index] * TILE_COLS + b_panel_cols[b_index]
                slot_index = slot_table[cell_index]
                usable = pair_iota < counts[row_pos, col_pos, layer_pos, step_pos]
                weights = ((slot_index[:, None] == slot_iota[None, :]) & usable[:, None]).astype(jnp.float32)
                running = running + jnp.dot(weights.T, products.reshape(PAIRS, BLOCK * BLOCK),
                                            precision=lax.Precision.HIGHEST)
        return running.reshape(KEPT, BLOCK, BLOCK)

    tiles = lax.map(compute_tile, jnp.arange(N_ROWS * N_COLS, dtype=jnp.int32))
    return tiles.reshape(N_ROWS, N_COLS, KEPT, BLOCK, BLOCK)
```

```python
import functools

import jax
import jax.numpy as jnp
from jax import lax
from jax.experimental import pallas as pl
from jax.experimental.pallas import tpu as pltpu
from jax.sharding import PartitionSpec as P

TILE_COLS = 8
KEPT = 48
CHUNKS = (26, 6)
UNROLL = 4


def from_behind(value, axis, by=1):
    peers = lax.axis_size(axis)
    return lax.ppermute(value, axis, [(i, (i + by) % peers) for i in range(peers)])


def split(block):
    high = block.astype(jnp.bfloat16)
    low = (block - high.astype(jnp.float32)).astype(jnp.bfloat16)
    return high, low


def product(left, right):
    left_high, left_low = split(left)
    right_high, right_low = split(right)
    lefts = jnp.concatenate([left_high, left_low], axis=1)
    rights = jnp.concatenate([right_high, right_low], axis=1)
    rights = jnp.concatenate([rights, rights], axis=0)
    both = jnp.dot(lefts, rights, preferred_element_type=jnp.float32)
    return both[:, : left.shape[1]] + both[:, left.shape[1] :]


def add_products(first, last, *refs):
    tables, kept, panels, (seed, out, work, total) = refs[:2], refs[2], refs[3:7], refs[7:]
    a_panels, b_panels = panels[:2], panels[2:]
    slots = out.shape[0]
    a_count, b_count = 32, b_panels[0].shape[0]
    pair_count = (tables[0].shape[0] - 1 - a_count - b_count) // 2
    base = lax.axis_index("layers") * slots
    width = out.shape[1]
    if seed is None:
        total[...] = jnp.zeros_like(total)
    else:
        total[:slots] = seed[...]
    total[slots] = jnp.zeros((width, width), jnp.float32)

    for side in range(2):
        table, a_ref, b_ref = tables[side], a_panels[side], b_panels[side]

        def scan(q, found):
            i = table[1 + a_count + b_count + q]
            j = table[1 + a_count + b_count + pair_count + q]
            slot = kept[table[1 + i] * TILE_COLS + table[1 + a_count + j]] - base
            use = (slot >= 0) & (slot < slots) & (i >= first) & (i < last)
            work[0, found] = i - first
            work[1, found] = j
            work[2, found] = slot
            return found + use.astype(jnp.int32)

        found = lax.fori_loop(0, table[0], scan, 0)
        for extra in range(UNROLL):
            work[0, found + extra] = 0
            work[1, found + extra] = 0
            work[2, found + extra] = slots

        def step(turn, carry):
            places = [turn * UNROLL + u for u in range(UNROLL)]
            values = [product(a_ref[work[0, p]], b_ref[work[1, p]]) for p in places]
            for p, value in zip(places, values):
                total[work[2, p]] += value
            return carry

        lax.fori_loop(0, (found + UNROLL - 1) // UNROLL, step, 0)
    out[...] = total[:slots]


def accumulate(first, last, tables, kept, a_panels, b_panels, seed):
    width = a_panels[0].shape[-1]
    slots = KEPT // lax.axis_size("layers")
    smem, vmem = pl.BlockSpec(memory_space=pltpu.SMEM), pl.BlockSpec(memory_space=pltpu.VMEM)
    operands = [*tables, kept, *a_panels, *b_panels] + ([] if seed is None else [seed])
    pairs = (tables[0].shape[0] - 1 - 32 - b_panels[0].shape[0]) // 2

    def body(*refs):
        if seed is None:
            refs = refs[:7] + (None,) + refs[7:]
        add_products(first, last, *refs)

    return pl.pallas_call(
        body,
        out_shape=jax.ShapeDtypeStruct((slots, width, width), jnp.float32),
        in_specs=[smem] * 3 + [vmem] * (len(operands) - 3),
        out_specs=vmem,
        scratch_shapes=[
            pltpu.SMEM((3, pairs + UNROLL), jnp.int32),
            pltpu.VMEM((slots + 1, width, width), jnp.float32),
        ],
        compiler_params=pltpu.CompilerParams(vmem_limit_bytes=32 << 20),
        cost_estimate=pl.CostEstimate(flops=10**9, bytes_accessed=6 << 20, transcendentals=0),
    )(*operands)


def on_device(a_blocks, a_rows, b_blocks, b_cols, pairs, counts, kept):
    a_own, b_own = a_blocks[0, 0, 0], b_blocks[0, 0, 0]
    rows_own, cols_own = a_rows[0, 0, 0], b_cols[0, 0, 0]
    pair_table, live = pairs[0, 0, 0], counts[0, 0, 0]
    slot_table = kept[0, 0].reshape(-1)

    def table(step, rows, cols):
        return jnp.concatenate([live[step : step + 1], rows, cols, pair_table[step].reshape(-1)])

    def with_other(value):
        return value, from_behind(value, "layers")

    rows_next = from_behind(rows_own, "rows")
    cols_next = from_behind(cols_own, "cols")
    chunks, start = [], 0
    for size in CHUNKS:
        chunks.append((start, from_behind(a_own[start : start + size], "rows")))
        start += size
    b_next = with_other(from_behind(b_own, "cols"))
    sums = accumulate(
        0, 32,
        with_other(table(0, rows_own, cols_own)),
        slot_table, with_other(a_own), with_other(b_own), None,
    )
    tables = with_other(table(1, rows_next, cols_next))
    for start, chunk in chunks:
        sums = accumulate(
            start, start + chunk.shape[0], tables, slot_table, with_other(chunk), b_next, sums
        )
    return sums[None, None]


def solution(mesh):
    return jax.shard_map(
        on_device,
        mesh=mesh,
        in_specs=(
            P(("parts", "rows"), "cols", "layers", None, None, None),
            P(("parts", "rows"), "cols", "layers", None),
            P(("parts", "rows"), "cols", "layers", None, None, None),
            P(("parts", "rows"), "cols", "layers", None),
            P(("parts", "rows"), "cols", "layers", None, None, None),
            P(("parts", "rows"), "cols", "layers", None),
            P(("parts", "rows"), "cols", None, None),
        ),
        out_specs=P(("parts", "rows"), "cols", "layers", None, None),
        check_vma=False,
    )
```

```python
import functools

import jax
import jax.numpy as jnp
from jax import lax
from jax.experimental import pallas as pl
from jax.experimental.pallas import tpu as pltpu
from jax.sharding import PartitionSpec as P

TILE_COLS = 8
KEPT = 48
A_BLOCKS = 32
B_BLOCKS = 8
CHUNKS = (25, 7)
UNROLL = 4


def from_behind(value, axis, by=1):
    peers = lax.axis_size(axis)
    return lax.ppermute(value, axis, [(i, (i + by) % peers) for i in range(peers)])


def split(block):
    high = block.astype(jnp.bfloat16)
    low = (block - high.astype(jnp.float32)).astype(jnp.bfloat16)
    return high, low


def product(left, right):
    left_high, left_low = split(left)
    right_high, right_low = split(right)
    lefts = jnp.concatenate([left_high, left_low], axis=1)
    rights = jnp.concatenate([right_high, right_low], axis=1)
    rights = jnp.concatenate([rights, rights], axis=0)
    both = jnp.dot(lefts, rights, preferred_element_type=jnp.float32)
    return both[:, : left.shape[1]] + both[:, left.shape[1] :]


def find(bounds, slots, own, other, kept, lists):
    base = lax.axis_index("layers") * slots
    chunk_count = len(bounds) - 1
    for row in range(2 * (chunk_count + 1)):
        lists[row, 0] = 0
    for side, table in enumerate((own, other)):
        pairs_at = 1 + A_BLOCKS + B_BLOCKS
        pair_count = (table.shape[0] - pairs_at) // 2

        def scan(q, carry):
            i = table[pairs_at + q]
            j = table[pairs_at + pair_count + q]
            slot = kept[table[1 + i] * TILE_COLS + table[1 + A_BLOCKS + j]] - base
            chunk = jnp.int32(0)
            first = jnp.int32(0)
            for low, high in zip(bounds[1:-1], bounds[1:-1]):
                chunk = chunk + (i >= low).astype(jnp.int32)
                first = jnp.where(i >= low, high, first)
            use = (slot >= 0) & (slot < slots)
            row = 2 * jnp.where(use, chunk, chunk_count) + side
            place = lists[row, 0] + 1
            lists[row, 0] = place
            lists[row, place] = (i - first) + 64 * j + 1024 * jnp.where(use, slot, slots)
            return carry

        lax.fori_loop(0, table[0], scan, 0)
    for row in range(2 * chunk_count):
        end = lists[row, 0] + 1
        for extra in range(UNROLL):
            lists[row, end + extra] = 1024 * slots


def find_pairs(bounds, tables, kept):
    slots = KEPT // lax.axis_size("layers")
    smem = pl.BlockSpec(memory_space=pltpu.SMEM)
    rows = 2 * len(bounds)
    return pl.pallas_call(
        functools.partial(find, bounds, slots),
        out_shape=jax.ShapeDtypeStruct((rows, 128), jnp.int32),
        in_specs=[smem] * 3,
        out_specs=smem,
        cost_estimate=pl.CostEstimate(flops=10**6, bytes_accessed=1 << 20, transcendentals=0),
    )(*tables, kept)


def add_products(chunk, lists, *refs):
    panels, (seed, out, total) = refs[:4], refs[4:]
    slots, width = out.shape[0], out.shape[1]
    if seed is None:
        total[...] = jnp.zeros_like(total)
    else:
        total[:slots] = seed[...]
        total[slots] = jnp.zeros((width, width), jnp.float32)
    for side in range(2):
        a_ref, b_ref = panels[side], panels[2 + side]
        row = 2 * chunk + side

        def step(turn, carry):
            codes = [lists[row, 1 + turn * UNROLL + u] for u in range(UNROLL)]
            values = [product(a_ref[code & 63], b_ref[(code >> 6) & 15]) for code in codes]
            for code, value in zip(codes, values):
                total[code >> 10] += value
            return carry

        lax.fori_loop(0, (lists[row, 0] + UNROLL - 1) // UNROLL, step, 0)
    out[...] = total[:slots]


def accumulate(chunk, lists, a_panels, b_panels, seed):
    width = a_panels[0].shape[-1]
    slots = KEPT // lax.axis_size("layers")
    smem, vmem = pl.BlockSpec(memory_space=pltpu.SMEM), pl.BlockSpec(memory_space=pltpu.VMEM)
    operands = [lists, *a_panels, *b_panels] + ([] if seed is None else [seed])

    def body(*refs):
        if seed is None:
            refs = refs[:5] + (None,) + refs[5:]
        add_products(chunk, *refs)

    return pl.pallas_call(
        body,
        out_shape=jax.ShapeDtypeStruct((slots, width, width), jnp.float32),
        in_specs=[smem] + [vmem] * (len(operands) - 1),
        out_specs=vmem,
        scratch_shapes=[pltpu.VMEM((slots + 1, width, width), jnp.float32)],
        compiler_params=pltpu.CompilerParams(vmem_limit_bytes=32 << 20),
        cost_estimate=pl.CostEstimate(flops=10**9, bytes_accessed=6 << 20, transcendentals=0),
    )(*operands)


def on_device(a_blocks, a_rows, b_blocks, b_cols, pairs, counts, kept):
    a_own, b_own = a_blocks[0, 0, 0], b_blocks[0, 0, 0]
    rows_own, cols_own = a_rows[0, 0, 0], b_cols[0, 0, 0]
    pair_table, live = pairs[0, 0, 0], counts[0, 0, 0]
    slot_table = kept[0, 0].reshape(-1)

    def table(step, rows, cols):
        return jnp.concatenate([live[step : step + 1], rows, cols, pair_table[step].reshape(-1)])

    def with_other(value):
        return value, from_behind(value, "layers")

    rows_next = from_behind(rows_own, "rows")
    bounds = (0,)
    for size in CHUNKS:
        bounds += (bounds[-1] + size,)
    pieces = [a_own[s:e] for s, e in zip(bounds, bounds[1:])]
    pieces[0], rows_next = lax.optimization_barrier((pieces[0], rows_next))
    chunks = [from_behind(pieces[0], "rows")]
    b_next = from_behind(b_own, "cols")
    cols_next = from_behind(cols_own, "cols")
    tables = with_other(table(0, rows_own, cols_own))
    lists = find_pairs((0, A_BLOCKS), tables, slot_table)
    sums = accumulate(0, lists, with_other(a_own), with_other(b_own), None)
    rows_next, cols_next, b_next, sums = lax.optimization_barrier(
        (rows_next, cols_next, b_next, sums)
    )
    b_next = with_other(b_next)
    tables = with_other(table(1, rows_next, cols_next))
    lists = find_pairs(bounds, tables, slot_table)
    chunk, piece, lists, sums = lax.optimization_barrier((chunks[0], pieces[1], lists, sums))
    last = from_behind(piece, "rows")
    sums = accumulate(0, lists, with_other(chunk), b_next, sums)
    last, sums = lax.optimization_barrier((last, sums))
    sums = accumulate(1, lists, with_other(last), b_next, sums)
    return sums[None, None]


def solution(mesh):
    return jax.shard_map(
        on_device,
        mesh=mesh,
        in_specs=(
            P(("parts", "rows"), "cols", "layers", None, None, None),
            P(("parts", "rows"), "cols", "layers", None),
            P(("parts", "rows"), "cols", "layers", None, None, None),
            P(("parts", "rows"), "cols", "layers", None),
            P(("parts", "rows"), "cols", "layers", None, None, None),
            P(("parts", "rows"), "cols", "layers", None),
            P(("parts", "rows"), "cols", None, None),
        ),
        out_specs=P(("parts", "rows"), "cols", "layers", None, None),
        check_vma=False,
    )
```

```python
import functools

import jax
import jax.numpy as jnp
from jax import lax
from jax.experimental import pallas as pl
from jax.experimental.pallas import tpu as pltpu
from jax.sharding import PartitionSpec as P

TILE_COLS = 8
KEPT = 48
A_BLOCKS = 32
B_BLOCKS = 8
CHUNKS = (18, 14)
UNROLL = 4


def from_behind(value, axis, by=1):
    peers = lax.axis_size(axis)
    return lax.ppermute(value, axis, [(i, (i + by) % peers) for i in range(peers)])


def split(block):
    high = block.astype(jnp.bfloat16)
    low = (block - high.astype(jnp.float32)).astype(jnp.bfloat16)
    return high, low


def product(left, right):
    left_high, left_low = split(left)
    right_high, right_low = split(right)
    lefts = jnp.concatenate([left_high, left_low], axis=1)
    rights = jnp.concatenate([right_high, right_low], axis=1)
    rights = jnp.concatenate([rights, rights], axis=0)
    both = jnp.dot(lefts, rights, preferred_element_type=jnp.float32)
    return both[:, : left.shape[1]] + both[:, left.shape[1] :]


def find(bounds, slots, own, other, kept, lists):
    base = lax.axis_index("layers") * slots
    chunk_count = len(bounds) - 1
    for row in range(2 * (chunk_count + 1)):
        lists[row, 0] = 0
    for side, table in enumerate((own, other)):
        pairs_at = 1 + A_BLOCKS + B_BLOCKS
        pair_count = (table.shape[0] - pairs_at) // 2

        def scan(q, carry):
            i = table[pairs_at + q]
            j = table[pairs_at + pair_count + q]
            slot = kept[table[1 + i] * TILE_COLS + table[1 + A_BLOCKS + j]] - base
            chunk = jnp.int32(0)
            first = jnp.int32(0)
            for low, high in zip(bounds[1:-1], bounds[1:-1]):
                chunk = chunk + (i >= low).astype(jnp.int32)
                first = jnp.where(i >= low, high, first)
            use = (slot >= 0) & (slot < slots)
            row = 2 * jnp.where(use, chunk, chunk_count) + side
            place = lists[row, 0] + 1
            lists[row, 0] = place
            lists[row, place] = (i - first) + 64 * j + 1024 * jnp.where(use, slot, slots)
            return carry

        lax.fori_loop(0, table[0], scan, 0)
    for row in range(2 * chunk_count):
        end = lists[row, 0] + 1
        for extra in range(UNROLL):
            lists[row, end + extra] = 1024 * slots


def find_pairs(bounds, tables, kept):
    slots = KEPT // lax.axis_size("layers")
    smem = pl.BlockSpec(memory_space=pltpu.SMEM)
    rows = 2 * len(bounds)
    return pl.pallas_call(
        functools.partial(find, bounds, slots),
        out_shape=jax.ShapeDtypeStruct((rows, 128), jnp.int32),
        in_specs=[smem] * 3,
        out_specs=smem,
        cost_estimate=pl.CostEstimate(flops=1, bytes_accessed=1, transcendentals=0),
    )(*tables, kept)


def add_products(chunk, lists, *refs):
    panels, (seed, out, total) = refs[:4], refs[4:]
    slots, width = out.shape[0], out.shape[1]
    if seed is None:
        total[...] = jnp.zeros_like(total)
    else:
        total[:slots] = seed[...]
        total[slots] = jnp.zeros((width, width), jnp.float32)
    for side in range(2):
        a_ref, b_ref = panels[side], panels[2 + side]
        row = 2 * chunk + side

        def step(turn, carry):
            codes = [lists[row, 1 + turn * UNROLL + u] for u in range(UNROLL)]
            values = [product(a_ref[code & 63], b_ref[(code >> 6) & 15]) for code in codes]
            for code, value in zip(codes, values):
                total[code >> 10] += value
            return carry

        lax.fori_loop(0, (lists[row, 0] + UNROLL - 1) // UNROLL, step, 0)
    out[...] = total[:slots]


def accumulate(chunk, lists, a_panels, b_panels, seed):
    width = a_panels[0].shape[-1]
    slots = KEPT // lax.axis_size("layers")
    smem, vmem = pl.BlockSpec(memory_space=pltpu.SMEM), pl.BlockSpec(memory_space=pltpu.VMEM)
    operands = [lists, *a_panels, *b_panels] + ([] if seed is None else [seed])

    def body(*refs):
        if seed is None:
            refs = refs[:5] + (None,) + refs[5:]
        add_products(chunk, *refs)

    return pl.pallas_call(
        body,
        out_shape=jax.ShapeDtypeStruct((slots, width, width), jnp.float32),
        in_specs=[smem] + [vmem] * (len(operands) - 1),
        out_specs=vmem,
        scratch_shapes=[pltpu.VMEM((slots + 1, width, width), jnp.float32)],
        compiler_params=pltpu.CompilerParams(vmem_limit_bytes=32 << 20),
        cost_estimate=pl.CostEstimate(flops=1, bytes_accessed=1, transcendentals=0),
    )(*operands)


def on_device(a_blocks, a_rows, b_blocks, b_cols, pairs, counts, kept):
    a_own, b_own = a_blocks[0, 0, 0], b_blocks[0, 0, 0]
    rows_own, cols_own = a_rows[0, 0, 0], b_cols[0, 0, 0]
    pair_table, live = pairs[0, 0, 0], counts[0, 0, 0]
    slot_table = kept[0, 0].reshape(-1)

    def table(step, rows, cols):
        return jnp.concatenate([live[step : step + 1], rows, cols, pair_table[step].reshape(-1)])

    def with_other(value):
        return value, from_behind(value, "layers")

    rows_next = from_behind(rows_own, "rows")
    bounds = (0,)
    for size in CHUNKS:
        bounds += (bounds[-1] + size,)
    pieces = [a_own[s:e] for s, e in zip(bounds, bounds[1:])]
    pieces[0], rows_next = lax.optimization_barrier((pieces[0], rows_next))
    chunks = [from_behind(pieces[0], "rows")]
    def other(value, *earlier):
        value = lax.optimization_barrier((value, *earlier))[0]
        return from_behind(value, "layers")

    own_table = table(0, rows_own, cols_own)
    other_table = other(own_table)
    a_other = other(a_own, rows_next)
    b_other = other(b_own, a_other)
    cols_in = lax.optimization_barrier((cols_own, rows_next))[0]
    cols_next = from_behind(cols_in, "cols")
    b_next = from_behind(b_own, "cols")
    piece = lax.optimization_barrier((pieces[1], other_table))[0]
    chunks.append(from_behind(piece, "rows"))
    lists = find_pairs((0, A_BLOCKS), (own_table, other_table), slot_table)
    sums = accumulate(0, lists, (a_own, a_other), (b_own, b_other), None)
    rows_next, cols_next, b_next, sums = lax.optimization_barrier(
        (rows_next, cols_next, b_next, sums)
    )
    b_next = with_other(b_next)
    tables = with_other(table(1, rows_next, cols_next))
    lists = find_pairs(bounds, tables, slot_table)
    chunk, last, lists, sums = *chunks, lists, sums
    chunk, lists, sums = lax.optimization_barrier((chunk, lists, sums))
    half = chunk.shape[0] // 2
    chunk_other = jnp.concatenate([other(chunk[:half]), other(chunk[half:])])
    sums = accumulate(0, lists, (chunk, chunk_other), b_next, sums)
    last, sums = lax.optimization_barrier((last, sums))
    sums = accumulate(1, lists, with_other(last), b_next, sums)
    return sums[None, None]


def solution(mesh):
    return jax.shard_map(
        on_device,
        mesh=mesh,
        in_specs=(
            P(("parts", "rows"), "cols", "layers", None, None, None),
            P(("parts", "rows"), "cols", "layers", None),
            P(("parts", "rows"), "cols", "layers", None, None, None),
            P(("parts", "rows"), "cols", "layers", None),
            P(("parts", "rows"), "cols", "layers", None, None, None),
            P(("parts", "rows"), "cols", "layers", None),
            P(("parts", "rows"), "cols", None, None),
        ),
        out_specs=P(("parts", "rows"), "cols", "layers", None, None),
        check_vma=False,
    )
```

```python
import functools

import jax
import jax.numpy as jnp
from jax import lax
from jax.experimental import pallas as pl
from jax.experimental.pallas import tpu as pltpu
from jax.sharding import PartitionSpec as P

TILE_COLS = 8
KEPT = 48
A_BLOCKS = 32
B_BLOCKS = 8
CHUNKS = (21, 11)
UNROLL = 8


def from_behind(value, axis, by=1):
    peers = lax.axis_size(axis)
    return lax.ppermute(value, axis, [(i, (i + by) % peers) for i in range(peers)])


def split(block):
    high = block.astype(jnp.bfloat16)
    low = (block - high.astype(jnp.float32)).astype(jnp.bfloat16)
    return high, low


def product(left, right):
    left_high, left_low = split(left)
    right_high, right_low = split(right)
    lefts = jnp.concatenate([left_high, left_low], axis=1)
    rights = jnp.concatenate([right_high, right_low], axis=1)
    rights = jnp.concatenate([rights, rights], axis=0)
    both = jnp.dot(lefts, rights, preferred_element_type=jnp.float32)
    return both[:, : left.shape[1]] + both[:, left.shape[1] :]


def find(bounds, slots, own, other, kept, lists):
    base = lax.axis_index("layers") * slots
    chunk_count = len(bounds) - 1
    for row in range(2 * (chunk_count + 1)):
        lists[row, 0] = 0
    for side, table in enumerate((own, other)):
        pairs_at = 1 + A_BLOCKS + B_BLOCKS
        pair_count = (table.shape[0] - pairs_at) // 2

        def scan(q, carry):
            i = table[pairs_at + q]
            j = table[pairs_at + pair_count + q]
            slot = kept[table[1 + i] * TILE_COLS + table[1 + A_BLOCKS + j]] - base
            chunk = jnp.int32(0)
            first = jnp.int32(0)
            for low, high in zip(bounds[1:-1], bounds[1:-1]):
                chunk = chunk + (i >= low).astype(jnp.int32)
                first = jnp.where(i >= low, high, first)
            use = (slot >= 0) & (slot < slots)
            row = 2 * jnp.where(use, chunk, chunk_count) + side
            place = lists[row, 0] + 1
            lists[row, 0] = place
            lists[row, place] = (i - first) + 64 * j + 1024 * jnp.where(use, slot, slots)
            return carry

        lax.fori_loop(0, table[0], scan, 0)
    for row in range(2 * chunk_count):
        end = lists[row, 0] + 1
        for extra in range(UNROLL):
            lists[row, end + extra] = 1024 * slots


def find_pairs(bounds, tables, kept):
    slots = KEPT // lax.axis_size("layers")
    smem = pl.BlockSpec(memory_space=pltpu.SMEM)
    rows = 2 * len(bounds)
    return pl.pallas_call(
        functools.partial(find, bounds, slots),
        out_shape=jax.ShapeDtypeStruct((rows, 128), jnp.int32),
        in_specs=[smem] * 3,
        out_specs=smem,
        cost_estimate=pl.CostEstimate(flops=1, bytes_accessed=1, transcendentals=0),
    )(*tables, kept)


def add_products(chunk, lists, *refs):
    panels, (seed, out, total) = refs[:4], refs[4:]
    slots, width = out.shape[0], out.shape[1]
    if seed is None:
        total[...] = jnp.zeros_like(total)
    else:
        total[:slots] = seed[...]
        total[slots] = jnp.zeros((width, width), jnp.float32)
    for side in range(2):
        a_ref, b_ref = panels[side], panels[2 + side]
        row = 2 * chunk + side

        def step(turn, carry):
            codes = [lists[row, 1 + turn * UNROLL + u] for u in range(UNROLL)]
            values = [product(a_ref[code & 63], b_ref[(code >> 6) & 15]) for code in codes]
            for code, value in zip(codes, values):
                total[code >> 10] += value
            return carry

        lax.fori_loop(0, (lists[row, 0] + UNROLL - 1) // UNROLL, step, 0)
    out[...] = total[:slots]


def accumulate(chunk, lists, a_panels, b_panels, seed):
    width = a_panels[0].shape[-1]
    slots = KEPT // lax.axis_size("layers")
    smem, vmem = pl.BlockSpec(memory_space=pltpu.SMEM), pl.BlockSpec(memory_space=pltpu.VMEM)
    operands = [lists, *a_panels, *b_panels] + ([] if seed is None else [seed])

    def body(*refs):
        if seed is None:
            refs = refs[:5] + (None,) + refs[5:]
        add_products(chunk, *refs)

    return pl.pallas_call(
        body,
        out_shape=jax.ShapeDtypeStruct((slots, width, width), jnp.float32),
        in_specs=[smem] + [vmem] * (len(operands) - 1),
        out_specs=vmem,
        scratch_shapes=[pltpu.VMEM((slots + 1, width, width), jnp.float32)],
        compiler_params=pltpu.CompilerParams(vmem_limit_bytes=32 << 20),
        cost_estimate=pl.CostEstimate(flops=1, bytes_accessed=1, transcendentals=0),
    )(*operands)


def on_device(a_blocks, a_rows, b_blocks, b_cols, pairs, counts, kept):
    a_own, b_own = a_blocks[0, 0, 0], b_blocks[0, 0, 0]
    rows_own, cols_own = a_rows[0, 0, 0], b_cols[0, 0, 0]
    pair_table, live = pairs[0, 0, 0], counts[0, 0, 0]
    slot_table = kept[0, 0].reshape(-1)

    def table(step, rows, cols):
        return jnp.concatenate([live[step : step + 1], rows, cols, pair_table[step].reshape(-1)])

    def with_other(value):
        return value, from_behind(value, "layers")

    rows_next = from_behind(rows_own, "rows")
    bounds = (0,)
    for size in CHUNKS:
        bounds += (bounds[-1] + size,)
    pieces = [a_own[s:e] for s, e in zip(bounds, bounds[1:])]
    pieces[0], rows_next = lax.optimization_barrier((pieces[0], rows_next))
    chunks = [from_behind(pieces[0], "rows")]
    def other(value, *earlier):
        value = lax.optimization_barrier((value, *earlier))[0]
        return from_behind(value, "layers")

    own_table = table(0, rows_own, cols_own)
    other_table = other(own_table)
    a_other = other(a_own, rows_next)
    b_other = other(b_own, a_other)
    cols_in = lax.optimization_barrier((cols_own, rows_next))[0]
    cols_next = from_behind(cols_in, "cols")
    b_next = from_behind(b_own, "cols")
    piece = lax.optimization_barrier((pieces[1], other_table))[0]
    chunks.append(from_behind(piece, "rows"))
    lists = find_pairs((0, A_BLOCKS), (own_table, other_table), slot_table)
    sums = accumulate(0, lists, (a_own, a_other), (b_own, b_other), None)
    rows_next, cols_next, b_next, sums = lax.optimization_barrier(
        (rows_next, cols_next, b_next, sums)
    )
    b_next = with_other(b_next)
    tables = with_other(table(1, rows_next, cols_next))
    lists = find_pairs(bounds, tables, slot_table)
    chunk, last, lists, sums = *chunks, lists, sums
    chunk, lists, sums = lax.optimization_barrier((chunk, lists, sums))
    third = chunk.shape[0] // 3
    cuts = (0, third, 2 * third, chunk.shape[0])
    chunk_other = jnp.concatenate([other(chunk[s:e]) for s, e in zip(cuts, cuts[1:])])
    sums = accumulate(0, lists, (chunk, chunk_other), b_next, sums)
    last, sums = lax.optimization_barrier((last, sums))
    sums = accumulate(1, lists, with_other(last), b_next, sums)
    return sums[None, None]


def solution(mesh):
    return jax.shard_map(
        on_device,
        mesh=mesh,
        in_specs=(
            P(("parts", "rows"), "cols", "layers", None, None, None),
            P(("parts", "rows"), "cols", "layers", None),
            P(("parts", "rows"), "cols", "layers", None, None, None),
            P(("parts", "rows"), "cols", "layers", None),
            P(("parts", "rows"), "cols", "layers", None, None, None),
            P(("parts", "rows"), "cols", "layers", None),
            P(("parts", "rows"), "cols", None, None),
        ),
        out_specs=P(("parts", "rows"), "cols", "layers", None, None),
        check_vma=False,
    )
```
